256 devices in a mesh: dp: 32 (over x, y, core), mp: 8 (over z).
Axes of the slice: x: 4, y: 4, z: 8, core: 2. Of those that a mesh axis runs over, the one named last changes fastest.
Arguments:
- hidden: bfloat16 [4096, 16384], P('dp', 'mp'), may hold values from -6 to 6
- weight: bfloat16 [16384, 8192], P('mp', 'dp'), may hold values from -0.20390625 to 0.20390625
- scale_param: float32 [16384], P('mp'), may hold values from 0.5 to 2
- clip_upper: float32 [8192], P('dp'), may hold values from 1 to 4
- clip_lower: float32 [8192], P('dp'), may hold values from 1 to 4
- target: bfloat16 [4096, 8192], P('mp', 'dp'), may hold values from -6 to 6
Outputs:
- approx: bfloat16 [4096, 8192], P('mp', 'dp')
- loss_value: float32 [], replicated
- grad_upper: float32 [8192], P('dp')
- grad_lower: float32 [8192], P('dp')
- grad_scale: float32 [16384], P('mp')
The draws below stay inside these ranges and needn't reach their ends.
All inputs are finite; a program needn't handle non-finite values.
Results may differ from the reference program's by a relative error of at most 0.011.
Values may be sent and summed in bfloat16 or wider, within the bound.
A program may use at most 128 MiB of HBM per device.

```python
import math
import jax
import jax.numpy as jnp
from jax import lax

D = 8192
FF_W = 16384
TOKENS = 4096


def draw_weight(key, part):
    key = jax.random.fold_in(key, 11)
    key_rows, key_cols, key_body = jax.random.split(key, 3)
    row_scale = jnp.exp(jax.random.uniform(key_rows, (FF_W, 1), jnp.float32) * math.log(10.0)) / 4.6
    col_scale = jnp.exp(jax.random.uniform(key_cols, (1, D), jnp.float32, math.log(0.5), math.log(2.0)))
    entries = jax.random.truncated_normal(key_body, -6.0, 6.0, (FF_W, D), jnp.float32)
    return (entries * row_scale * col_scale / math.sqrt(FF_W)).astype(jnp.bfloat16)


def shard_levels(rng, dims, shards, smallest, high):
    def one(axis_at, parts):
        steps = jax.random.uniform(jax.random.fold_in(jax.random.fold_in(rng, 6), axis_at), (parts,), jnp.float32, smallest / len(shards), high / len(shards))
        return jnp.repeat(jnp.exp(steps), dims[axis_at] // parts).reshape((-1,) + (1,) * (len(dims) - axis_at - 1))

    level = one(*shards[0])
    for cut in shards[1:]:
        level = level * one(*cut)
    return level


def normal_values(key, shape, scale, bound, cuts=(), kind=jnp.bfloat16):
    values = jax.random.normal(key, shape, jnp.float32) * scale
    if len(cuts) > 0:
        values = shard_levels(key, shape, cuts, -0.22, 0.18) * values
    return jnp.clip(values, min=-bound, max=bound).astype(kind)


def setup_inputs(seed: int = 0) -> dict:
    key_list = jax.random.split(jax.random.key(seed), 7)
    return {
        "hidden": normal_values(key_list[0], (TOKENS, FF_W), 1.0, 6.0, ((0, 32), (1, 8))),
        "weight": draw_weight(jax.random.fold_in(key_list[6], 71), 0),
        "scale_param": jnp.clip(jnp.exp(math.log(2.0) - 1.3862944 * jax.random.uniform(key_list[2], (FF_W,), jnp.float32) ** shard_levels(key_list[2], (FF_W,), ((0, 8),), -0.2, 0.2)), 0.5, 2.0),
        "clip_upper": jnp.clip(1.0 + 3.0 * jax.random.uniform(key_list[3], (D,), jnp.float32) ** shard_levels(key_list[3], (D,), ((0, 32),), -0.2, 0.2), 1.0, 4.0),
        "clip_lower": jnp.clip(1.0 + 3.0 * jax.random.uniform(key_list[4], (D,), jnp.float32) ** shard_levels(key_list[4], (D,), ((0, 32),), -0.2, 0.2), 1.0, 4.0),
        "target": normal_values(key_list[5], (TOKENS, D), 1.0, 6.0, ((0, 8), (1, 32))),
    }


def quantize(wscaled, upper_logit, lower_logit, col_max, col_min):
    upper = jax.nn.sigmoid(upper_logit) * col_max
    lower = jax.nn.sigmoid(lower_logit) * col_min
    stepsize = (upper - lower + 1e-05) / 15.0
    level = jnp.clip((wscaled - lower) / stepsize, 0.0, 15.0)
    soft = level - 0.8 * jnp.sin(2.0 * math.pi * level) / (2.0 * math.pi)
    return stepsize * soft + lower

def reference(hidden, weight, scale_param, clip_upper, clip_lower, target):
    hprime = (hidden.astype(jnp.float32) / scale_param).astype(jnp.bfloat16)
    hwide = hprime.astype(jnp.float32)
    width = math.gcd(D, 512)
    blocks = D // width

    def one_block(carry, index):
        scale_acc, loss_acc = carry
        begin = (index * width).astype(jnp.int32)
        wraw = lax.dynamic_slice_in_dim(weight, begin, width, 1).astype(jnp.float32)
        upper_logit = lax.dynamic_slice_in_dim(clip_upper, begin, width, 0)
        lower_logit = lax.dynamic_slice_in_dim(clip_lower, begin, width, 0)
        goal = lax.dynamic_slice_in_dim(target, begin, width, 1).astype(jnp.float32)
        wscaled = wraw * scale_param[:, None]
        col_max = lax.optimization_barrier(jnp.max(wscaled, axis=0))
        col_min = lax.optimization_barrier(jnp.min(wscaled, axis=0))
        wquant = quantize(wscaled, upper_logit, lower_logit, col_max, col_min).astype(jnp.bfloat16)
        output = jnp.dot(hwide, wquant.astype(jnp.float32), precision=lax.Precision.HIGHEST)
        error = output - goal
        error_bf = error.astype(jnp.bfloat16)
        wgrad = lax.dot_general(hwide, error_bf.astype(jnp.float32), (((0,), (0,)), ((), ())), precision=lax.Precision.HIGHEST)
        unused, pullback = jax.vjp(lambda w, u, l: quantize(w, u, l, col_max, col_min), wscaled, upper_logit, lower_logit)
        dscaled, dupper, dlower = pullback(wgrad)
        scale_term = lax.optimization_barrier(jnp.sum(dscaled * wraw - wquant.astype(jnp.float32) * wgrad / scale_param[:, None], axis=1))
        return ((scale_acc + scale_term, loss_acc + jnp.sum(error * error)), (output.astype(jnp.bfloat16), dupper, dlower))
    start = (jnp.zeros((FF_W,), jnp.float32), jnp.zeros((), jnp.float32))
    (grad_scale, loss_total), (pieces, uppers, lowers) = lax.scan(one_block, start, jnp.arange(blocks, dtype=jnp.int32))
    approx = jnp.moveaxis(pieces, 0, 1).reshape(TOKENS, D)
    loss_value = loss_total / (TOKENS * D)
    return (approx, loss_value, uppers.reshape(D), lowers.reshape(D), grad_scale)
```

```python
import functools
import math

import jax
import jax.numpy as jnp
import numpy as np
from jax import lax
from jax.experimental import pallas as pl
from jax.experimental.pallas import tpu as pltpu
from jax.sharding import PartitionSpec as P

D = 8192
FF_W = 16384
TOKENS = 4096

X = 4
Z = 8
G = 4
TB = 32
HF = 1024
HD = 256
GT = X * X * 2 * TB
ZB = GT // Z
NH = 2
ZH = ZB // NH
COLUMN = 2 * Z
PLANE = X * X

f32 = jnp.float32
bf16 = jnp.bfloat16
MESH = pl.DeviceIdType.MESH


def rem(a, n):
    return lax.rem(a, jnp.int32(n))


def div(a, n):
    return lax.div(a, jnp.int32(n))


def in_squares(values, terms):
    nodes = 0.125 + 0.125 * np.cos(np.pi * (np.arange(64) + 0.5) / 64)
    fit = np.polynomial.chebyshev.Chebyshev.fit(nodes, values(nodes), terms - 1, domain=[0.0, 0.25])
    return [float(v) for v in fit.convert(kind=np.polynomial.Polynomial).coef[::-1]]


SINE = in_squares(lambda u: np.sin(2 * np.pi * np.sqrt(u)) / np.sqrt(u), 6)
COSINE = in_squares(lambda u: np.cos(2 * np.pi * np.sqrt(u)), 6)


def horner(coefs, u):
    v = coefs[0]
    for k in coefs[1:]:
        v = v * u + k
    return v


def kernel(
    hid, wgt, scl, cu, cl, tgt,
    apx, loss, gu_o, gl_o, gs_o,
    hall, hstage, wpeer, clipb, scol, wq, tU, tL, tS, red, colv, stat, part, pst, prc,
    sl, rl, ss, rs, eT, acc, gsacc, lacc, lossb, gradb, planeb, gsp,
    agS, agR, hxS, hxR, msS, msR, pS, pR, lS, lR, shS, shR, elS, elR, esS, esR, epS, epR,
    stS, stR, loS, loR, grS, grR, plS, plR,
):
    dp = lax.axis_index("dp")
    z = lax.axis_index("mp")
    c = rem(dp, 2)
    chip = div(dp, 2)
    x = div(chip, X)
    y = rem(chip, X)
    s = 1 - 2 * c
    column = z * 2 + c
    peer = (chip * 2 + 1 - c, z)
    around = {r: rem(z + Z + r * s, Z) for r in range(-4, 5)}

    def remote(src, dst, send, recv, device):
        return pltpu.make_async_remote_copy(
            src_ref=src, dst_ref=dst, send_sem=send, recv_sem=recv,
            device_id=device, device_id_type=MESH,
        )

    def in_column(o):
        other = rem(column + o, COLUMN)
        return (chip * 2 + rem(other, 2), div(other, 2))

    def in_plane(o):
        return (rem(chip + o, PLANE) * 2 + c, z)

    barrier = pltpu.get_barrier_semaphore()

    def greet(o, carry):
        pl.semaphore_signal(barrier, inc=1, device_id=in_column(o), device_id_type=MESH)
        pl.semaphore_signal(barrier, inc=1, device_id=in_plane(o), device_id_type=MESH)
        return carry

    lax.fori_loop(1, COLUMN, greet, 0)
    pl.semaphore_wait(barrier, COLUMN - 1 + PLANE - 1)

    mine = pl.ds(pl.multiple_of(c * HF, HF), HF)
    theirs = pl.ds(pl.multiple_of((1 - c) * HF, HF), HF)

    def h_copy(g):
        return remote(
            hstage.at[pl.ds(pl.multiple_of(g * TB, TB), TB), :], hall.at[g, x, y, c],
            hxS.at[g], hxR.at[g], peer,
        )

    def scale_hidden(g, carry):
        rows = pl.ds(pl.multiple_of(g * TB, TB), TB)
        there = (hid[rows, theirs].astype(f32) / scl[:, theirs]).astype(bf16)
        hstage[rows, :] = there
        h_copy(g).start()
        here = (hid[rows, mine].astype(f32) / scl[:, mine]).astype(bf16)
        hall[g, x, y, c] = here
        return carry

    scale_hidden(0, 0)
    w_copy = remote(wgt.at[theirs, :], wpeer, msS.at[0], msR.at[0], peer)
    w_copy.start()
    for b in range(2):
        clipb[c, b:b + 1, :] = cu[b:b + 1, :]
        clipb[c, 2 + b:3 + b, :] = cl[b:b + 1, :]
    clip_copy = remote(clipb.at[c], clipb.at[c], msS.at[1], msR.at[1], peer)
    clip_copy.start()

    def h_wait(g):
        slot = hall.at[g, x, y, 1 - c]
        remote(slot, slot, hxS.at[g], hxR.at[g], peer).wait_recv()

    xs = {o: rem(x + X + o * s, X) for o in (0, -1, 1, 2)}
    ys = {o: rem(y + X + o * s, X) for o in (0, -1, 1, 2)}
    x_way = {o: (xs[o] * X + y) * 2 + c for o in (-1, 1)}
    y_way = {o: (x * X + ys[o]) * 2 + c for o in (-1, 1)}

    def block(g, b, p, q):
        return hall.at[g, xs[p], ys[q], 0] if b == 0 else hall.at[g, xs[q], ys[p], 1]

    routes = [(0, 0, 0, 1, -1, 0), (0, 0, 0, -1, 1, 0), (-1, 0, 0, 1, 2, 0)]
    for p in (0, -1, 1, 2):
        routes += [(p, 0, 1, 1, p, -1), (p, 0, 1, -1, p, 1), (p, -1, 1, 1, p, 2)]

    def ag_start(g, b, k):
        p, q, axis, way, _, _ = routes[k]
        src = block(g, b, p, q)
        to = (x_way if axis == b else y_way)[way]
        remote(src, src, agS.at[g, b, k], agR.at[g, b, k], (to, z)).start()

    def ag_wait(g, b, k):
        dst = block(g, b, routes[k][4], routes[k][5])
        remote(dst, dst, agS.at[g, b, k], agR.at[g, b, k], peer).wait_recv()

    def ag_step(g, arrived, onward):
        for b in range(2):
            for k in arrived:
                ag_wait(g, b, k)
            for k in onward:
                ag_start(g, b, k)

    def ag_0(g):
        h_wait(g)
        ag_step(g, (), (0, 1, 3, 4))

    def ag_1(g):
        ag_step(g, (0,), (2, 6, 7))

    def ag_2(g):
        ag_step(g, (1,), (9, 10))
        ag_step(g, (2,), (12, 13))

    def ag_3(g):
        for k in (3, 6, 9, 12):
            ag_step(g, (k,), (k + 2,))

    def ag_4(g):
        ag_step(g, (4, 7, 10, 13, 5, 8, 11, 14), ())

    def ag_sent(g):
        def one(k, carry):
            for b in range(2):
                src = block(g, b, 0, 0)
                remote(src, src, agS.at[g, b, k], agR.at[g, b, k], peer).wait_send()
            return carry

        lax.fori_loop(0, 15, one, 0)

    ag_0(0)

    for k in range(2 * HF // 128):
        lanes = slice(128 * k, 128 * k + 128)
        scol[lanes, :] = jnp.broadcast_to(scl[:, lanes], (128, 128)).T

    def extremes(k, carry):
        rows = pl.ds(pl.multiple_of(k * 64, 64), 64)
        ws = wgt[rows, :].astype(f32) * jnp.concatenate([scol[rows, :]] * 2, axis=1)
        ws = ws.reshape(8, 8, HD)
        return jnp.maximum(carry[0], jnp.max(ws, axis=0)), jnp.minimum(carry[1], jnp.min(ws, axis=0))

    top, bottom = lax.fori_loop(
        0, 2 * HF // 64, extremes, (jnp.full((8, HD), -jnp.inf, f32), jnp.full((8, HD), jnp.inf, f32))
    )
    top = jnp.max(top, axis=0, keepdims=True)
    bottom = jnp.min(bottom, axis=0, keepdims=True)
    for r in range(2):
        stat[column, r:r + 1, :] = top[:, 128 * r:128 * r + 128]
        stat[column, 2 + r:3 + r, :] = bottom[:, 128 * r:128 * r + 128]

    def column_send(buf, send, recv):
        def one(o, carry):
            remote(buf.at[column], buf.at[column], send.at[o - 1], recv.at[o - 1], in_column(o)).start()
            return carry
        lax.fori_loop(1, COLUMN, one, 0)

    def column_wait(buf, send, recv):
        def one(o, carry):
            src = buf.at[rem(column + COLUMN - o, COLUMN)]
            remote(src, src, send.at[o - 1], recv.at[o - 1], peer).wait_recv()
            return carry
        lax.fori_loop(1, COLUMN, one, 0)

    def column_sent(buf, send, recv):
        def one(o, carry):
            src = buf.at[column]
            remote(src, src, send.at[o - 1], recv.at[o - 1], peer).wait_send()
            return carry
        lax.fori_loop(1, COLUMN, one, 0)

    column_send(stat, stS, stR)
    lax.fori_loop(1, G, scale_hidden, 0)
    ag_1(0)

    lacc[...] = jnp.zeros_like(lacc)
    acc[...] = jnp.zeros_like(acc)
    gsacc[...] = jnp.zeros_like(gsacc)

    clip_other = clipb.at[1 - c]
    remote(clip_other, clip_other, msS.at[1], msR.at[1], peer).wait_recv()
    column_wait(stat, stS, stR)
    every = stat[...].reshape(Z, 2, 8, 128)
    col_max = jnp.max(every[:, :, 0:2, :], axis=0).reshape(4, 128)
    col_min = jnp.min(every[:, :, 2:4, :], axis=0).reshape(4, 128)
    sig_u = jax.nn.sigmoid(jnp.concatenate([clipb[0, 0:2, :], clipb[1, 0:2, :]], axis=0))
    sig_l = jax.nn.sigmoid(jnp.concatenate([clipb[0, 2:4, :], clipb[1, 2:4, :]], axis=0))
    lower = sig_l * col_min
    stepsize = (sig_u * col_max - lower + 1e-05) / 15.0
    inverse = 1.0 / stepsize
    first = c == 0

    def own_rows(v):
        return jnp.where(first, v[0:2], v[2:4])

    def other_rows(v):
        return jnp.where(first, v[2:4], v[0:2])

    def levels(ws, lo, inv):
        raw = (ws - lo) * inv
        level = jnp.clip(raw, 0.0, 15.0)
        turn = level - jnp.floor(level + 0.5)
        square = turn * turn
        soft = level - turn * horner([v * (0.8 / (2.0 * math.pi)) for v in SINE], square)
        return raw, level, square, soft

    STRIP = 16

    def quantize(src, row0, half, pick):
        lo, inv, st = pick(lower), pick(inverse), pick(stepsize)

        def one(k, carry):
            rows = pl.ds(pl.multiple_of(k * STRIP, STRIP), STRIP)
            sc = scol[pl.ds(pl.multiple_of(c * HF + k * STRIP, STRIP), STRIP), :]
            w = src[pl.ds(pl.multiple_of(row0 + k * STRIP, STRIP), STRIP), :].astype(f32)
            for r in range(2):
                lanes = slice(128 * r, 128 * r + 128)
                _, _, _, soft = levels(w[:, lanes] * sc, lo[r:r + 1], inv[r:r + 1])
                wq[rows, half * HD + 128 * r:half * HD + 128 * r + 128] = (st[r:r + 1] * soft + lo[r:r + 1]).astype(bf16)
            return carry

        lax.fori_loop(0, HF // STRIP, one, 0)

    ag_2(0)
    ag_0(1)
    quantize(wgt, c * HF, 1, own_rows)
    ag_3(0)
    w_copy.wait_recv()
    quantize(wpeer, 0, 0, other_rows)
    ag_1(1)

    def columns():
        for r in range(4):
            rows = slice(128 * r, 128 * r + 128)
            for n, v in enumerate((lower, stepsize, inverse)):
                colv[n, rows, :] = jnp.broadcast_to(v[r:r + 1, :], (128, 128)).T

    def coefficients(k):
        lanes = pl.ds(pl.multiple_of(k * 128, 128), 128)
        sc = scl[:, pl.ds(pl.multiple_of(c * HF + k * 128, 128), 128)]
        rsc = 1.0 / sc
        for src, row0, core in ((wgt, c * HF, c), (wpeer, 0, 1 - c)):
            rows = pl.ds(pl.multiple_of(core * HD, HD), HD)
            tU[rows, lanes] = src[pl.ds(pl.multiple_of(row0 + k * 128, 128), 128), :].astype(f32).T

        def one(n, carry):
            rows = pl.ds(pl.multiple_of(n * 32, 32), 32)
            w = tU[rows, lanes]
            lo = colv[0, rows, :]
            raw, level, square, soft = levels(w * sc, lo, colv[2, rows, :])
            tie = jnp.where((raw == 0.0) | (raw == 15.0), 0.5, 1.0)
            inside = jnp.where(raw == level, tie, 0.0)
            slope = inside * (1.0 - 0.8 * horner(COSINE, square))
            q = (colv[1, rows, :] * soft + lo).astype(bf16).astype(f32)
            up = (soft - slope * level) * (1.0 / 15.0)
            tU[rows, lanes] = up
            tL[rows, lanes] = 1.0 - slope - up
            tS[rows, lanes] = slope * w - q * rsc
            return carry

        lax.fori_loop(0, 2 * HD // 32, one, 0)

    own_half = pl.ds(pl.multiple_of(c * HD, HD), HD)
    segments = [(jj * 2 * G * TB + b * G * TB, (2 * jj + b) * TB) for jj in range(2) for b in range(2)]
    MT = GT // 2

    def p_copy(g, t):
        part_of = pl.ds(4 * t, 4)
        return remote(pst.at[g, part_of], prc.at[g, part_of], pS.at[g, t], pR.at[g, t], peer)

    def forward(g):
        def one(t, carry):
            h = hall[g, pl.ds(2 * t, 2)].reshape(MT, HF)
            r = jnp.dot(h, wq[...], preferred_element_type=f32)
            for n in range(4):
                rows = slice(n * ZB, n * ZB + ZB)
                pst[g, 4 * t + n] = r[rows, :HD].astype(bf16)
                part[rem(g, 3), 4 * t + n] = r[rows, HD:]
            p_copy(g, t).start()
            return carry

        lax.fori_loop(0, 2, one, 0)

    def zcopy(src, dst, send, recv, to):
        return remote(src, dst, send, recv, (dp, to))

    def long_copy(g, m, h):
        n = (g, m - 1, h)
        return zcopy(sl.at[n], rl.at[n], lS.at[n], lR.at[n], around[1])

    def short_copy(g, m, h):
        n = (g, m - 1, h)
        return zcopy(ss.at[n], rs.at[n], shS.at[n], shR.at[n], around[-1])

    def total(g, block, h):
        rows = slice(h * ZH, h * ZH + ZH)
        return part[rem(g, 3), block, rows, :] + prc[g, block, rows, :].astype(f32)

    def sum_step(g, m):
        if m == 1:
            for t in range(2):
                p_copy(g, t).wait_recv()
        for h in range(NH):
            if m > 1:
                long_copy(g, m - 1, h).wait_recv()
            v = total(g, around[5 - m], h)
            if m > 1:
                v = v + rl[g, m - 2, h].astype(f32)
            sl[g, m - 1, h] = v.astype(bf16)
            long_copy(g, m, h).start()
            if m < 4:
                if m > 1:
                    short_copy(g, m - 1, h).wait_recv()
                v = total(g, around[m - 4], h)
                if m > 1:
                    v = v + rs[g, m - 2, h].astype(f32)
                ss[g, m - 1, h] = v.astype(bf16)
                short_copy(g, m, h).start()

    def eslot(g, block, core):
        return eT.at[g, block, pl.ds(pl.multiple_of(core * HD, HD), HD), :]

    def ehalf(g, block, h):
        return eT.at[g, block, pl.ds(pl.multiple_of(c * HD + h * (HD // NH), HD // NH), HD // NH), :]

    def long_err(g, m, h, recv=False):
        e = ehalf(g, around[-m if recv else 1 - m], h)
        return zcopy(e, e, elS.at[g, m - 1, h], elR.at[g, m - 1, h], around[1])

    def short_err(g, m, h, recv=False):
        e = ehalf(g, around[m if recv else m - 1], h)
        return zcopy(e, e, esS.at[g, m - 1, h], esR.at[g, m - 1, h], around[-1])

    def peer_err(g, block, core):
        e = eslot(g, block, core)
        return remote(e, e, epS.at[g, block], epR.at[g, block], peer)

    def err_step(g, m):
        for h in range(NH):
            long_err(g, m, h, True).wait_recv()
            if m < 4:
                long_err(g, m + 1, h).start()
                short_err(g, m, h, True).wait_recv()
                if m < 3:
                    short_err(g, m + 1, h).start()
        peer_err(g, around[-m], c).start()
        if m < 4:
            peer_err(g, around[m], c).start()

    def sum_end(g):
        for h in range(NH):
            long_copy(g, 4, h).wait_recv()
            short_copy(g, 3, h).wait_recv()
        v = jnp.concatenate(
            [total(g, z, h) + rl[g, 3, h].astype(f32) + rs[g, 2, h].astype(f32) for h in range(NH)], axis=0
        )
        goal = jnp.concatenate(
            [tgt[pl.ds(pl.multiple_of(first + g * TB, TB), TB), :] for first, _ in segments], axis=0
        ).astype(f32)
        err = v - goal
        eT[g, z, own_half, :] = err.T.astype(bf16)
        for h in range(NH):
            long_err(g, 1, h).start()
            short_err(g, 1, h).start()
        peer_err(g, z, c).start()
        lacc[...] += jnp.sum((err * err).reshape(ZB // 8, 8, HD), axis=0)
        back = v.astype(bf16)
        for first, at_row in segments:
            apx[pl.ds(pl.multiple_of(first + g * TB, TB), TB), :] = back[at_row:at_row + TB, :]

    def backward(g):
        def landed(block, carry):
            peer_err(g, block, 1 - c).wait_recv()
            return carry

        lax.fori_loop(0, Z, landed, 0)

        def one(k, carry):
            lanes = pl.ds(pl.multiple_of(k * 512, 512), 512)
            e = jnp.concatenate([eT[g, i] for i in range(Z)], axis=1)
            acc[:, lanes] += jnp.dot(
                e, hall[g, :, :, :, :, lanes].reshape(GT, 512), preferred_element_type=f32
            )
            return carry

        lax.fori_loop(0, HF // 512, one, 0)

    def z_sent(g):
        for h in range(NH):
            for m in range(1, 5):
                long_copy(g, m, h).wait_send()
                long_err(g, m, h).wait_send()
            for m in range(1, 4):
                short_copy(g, m, h).wait_send()
                short_err(g, m, h).wait_send()
        for t in range(2):
            p_copy(g, t).wait_send()

        def one(block, carry):
            peer_err(g, block, c).wait_send()
            return carry

        lax.fori_loop(0, Z, one, 0)

    def turn_of(i, carry):
        def when(back, f, *more):
            g = i - back

            @pl.when((g >= 0) & (g < G))
            def _():
                f(g, *more)

        when(0, ag_4)
        when(-1, ag_2)
        when(0, forward)
        when(-2, ag_0)

        when(4, err_step, 4)
        when(3, err_step, 2)
        when(2, sum_end)
        when(1, sum_step, 3)
        when(0, sum_step, 1)
        when(-1, ag_3)

        @pl.when(i == G + 1)
        def _():
            lossb[column] = lacc[:, 0:128] + lacc[:, 128:256]
            column_send(lossb, loS, loR)

        @pl.when(i == G - 1)
        def _():
            columns()

        @pl.when((i >= G - 1) & (i < G + 3))
        def _():
            coefficients(2 * (i - G + 1))

        when(3, err_step, 3)
        when(2, err_step, 1)
        when(1, sum_step, 4)
        when(0, sum_step, 2)
        when(-2, ag_1)

        @pl.when((i >= G - 1) & (i < G + 3))
        def _():
            coefficients(2 * (i - G + 1) + 1)

        when(4, ag_sent)
        when(4, backward)
        when(5, z_sent)
        return carry

    lax.fori_loop(0, G + 4, turn_of, 0)
    def pull(a, carry):
        rows = pl.ds(pl.multiple_of(a * 64, 64), 64)
        up = jnp.zeros((64, 128), f32)
        low = jnp.zeros((64, 128), f32)
        for k in range(HF // 128):
            lanes = slice(128 * k, 128 * k + 128)
            g = acc[rows, lanes]
            up = up + g * tU[rows, lanes]
            low = low + g * tL[rows, lanes]
            gsacc[:, lanes] += jnp.sum((g * tS[rows, lanes]).reshape(8, 8, 128), axis=0)
        red[0, rows, :] = up
        red[1, rows, :] = low
        return carry

    lax.fori_loop(0, 2 * HD // 64, pull, 0)
    column_wait(lossb, loS, loR)
    planeb[chip, 8:16, :] = jnp.sum(lossb[...], axis=0)
    gs_row = jnp.sum(gsacc[...], axis=0, keepdims=True)
    for k in range(HF // 128):
        planeb[chip, k:k + 1, :] = gs_row[:, 128 * k:128 * k + 128]

    def plane_copy(o, from_chip, device):
        src = planeb.at[from_chip]
        return remote(src, src, plS.at[o - 1], plR.at[o - 1], device)

    def plane_start(o, carry):
        plane_copy(o, chip, in_plane(o)).start()
        return carry

    lax.fori_loop(1, PLANE, plane_start, 0)

    for r in range(4):
        rows = slice(128 * r, 128 * r + 128)
        gradb[column, r:r + 1, :] = jnp.sum(red[0, rows, :].T, axis=0, keepdims=True)
        gradb[column, 4 + r:5 + r, :] = jnp.sum(red[1, rows, :].T, axis=0, keepdims=True)
    column_send(gradb, grS, grR)

    w_copy.wait_send()
    clip_copy.wait_send()

    def sent(g, carry):
        h_copy(g).wait_send()
        return carry

    lax.fori_loop(0, G, sent, 0)
    z_sent(G - 1)
    column_sent(stat, stS, stR)
    column_sent(lossb, loS, loR)

    def plane_wait(o, carry):
        plane_copy(o, rem(chip + PLANE - o, PLANE), peer).wait_recv()
        return carry

    lax.fori_loop(1, PLANE, plane_wait, 0)
    whole = jnp.sum(planeb[...], axis=0)
    gsp[c] = whole[0:8, :]
    gs_copy = remote(gsp.at[c], gsp.at[c], msS.at[2], msR.at[2], peer)
    gs_copy.start()
    loss[0, 0] = jnp.sum(whole[8:16, :]) * (1.0 / (TOKENS * D))

    column_wait(gradb, grS, grR)
    grads = jnp.sum(gradb[...], axis=0)
    su = own_rows(sig_u)
    sd = own_rows(sig_l)
    gu_o[...] = (
        jnp.where(first, grads[0:2], grads[2:4])
        * own_rows(col_max) * (su * (1.0 - su))
    )
    gl_o[...] = (
        jnp.where(first, grads[4:6], grads[6:8])
        * own_rows(col_min) * (sd * (1.0 - sd))
    )
    column_sent(gradb, grS, grR)

    def plane_sent(o, carry):
        plane_copy(o, chip, peer).wait_send()
        return carry

    lax.fori_loop(1, PLANE, plane_sent, 0)
    gs_other = gsp.at[1 - c]
    remote(gs_other, gs_other, msS.at[2], msR.at[2], peer).wait_recv()
    gs_copy.wait_send()
    gs_o[0:8, :] = gsp[0]
    gs_o[8:16, :] = gsp[1]


def hand_over(*refs):
    n = len(refs) // 2
    for i in range(n):
        refs[n + i][...] = refs[i][...]


def per_device(hidden, weight, scale_param, clip_upper, clip_lower, target):
    vmem = pl.BlockSpec(memory_space=pltpu.VMEM)
    dma = pltpu.SemaphoreType.DMA
    scratch = [
        pltpu.VMEM((G, X, X, 2, TB, HF), bf16),
        pltpu.VMEM((G * TB, HF), bf16),
        pltpu.VMEM((HF, HD), bf16),
        pltpu.VMEM((2, 8, 128), f32),
        pltpu.VMEM((2 * HF, 128), f32),
        pltpu.VMEM((HF, 2 * HD), bf16),
        pltpu.VMEM((2 * HD, HF), f32),
        pltpu.VMEM((2 * HD, HF), f32),
        pltpu.VMEM((2 * HD, HF), f32),
        pltpu.VMEM((2, 2 * HD, 128), f32),
        pltpu.VMEM((3, 2 * HD, 128), f32),
        pltpu.VMEM((COLUMN, 8, 128), f32),
        pltpu.VMEM((3, Z, ZB, HD), f32),
        pltpu.VMEM((G, Z, ZB, HD), bf16),
        pltpu.VMEM((G, Z, ZB, HD), bf16),
        pltpu.VMEM((G, 4, NH, ZH, HD), bf16),
        pltpu.VMEM((G, 4, NH, ZH, HD), bf16),
        pltpu.VMEM((G, 3, NH, ZH, HD), bf16),
        pltpu.VMEM((G, 3, NH, ZH, HD), bf16),
        pltpu.VMEM((G, Z, 2 * HD, ZB), bf16),
        pltpu.VMEM((2 * HD, HF), f32),
        pltpu.VMEM((8, HF), f32),
        pltpu.VMEM((8, HD), f32),
        pltpu.VMEM((COLUMN, 8, 128), f32),
        pltpu.VMEM((COLUMN, 8, 128), f32),
        pltpu.VMEM((PLANE, 16, 128), f32),
        pltpu.VMEM((2, 8, 128), f32),
    ]
    for shape in (
        (G, 2, 15), (G,), (3,), (G, 2), (G, 4, NH), (G, 3, NH), (G, 4, NH), (G, 3, NH), (G, Z),
        (COLUMN - 1,), (COLUMN - 1,), (COLUMN - 1,), (PLANE - 1,),
    ):
        scratch += [dma(shape), dma(shape)]
    shapes = (
        jax.ShapeDtypeStruct((TOKENS // Z, HD), bf16),
        jax.ShapeDtypeStruct((1, 1), f32),
        jax.ShapeDtypeStruct((2, 128), f32),
        jax.ShapeDtypeStruct((2, 128), f32),
        jax.ShapeDtypeStruct((16, 128), f32),
    )
    results = pl.pallas_call(
        kernel,
        out_shape=shapes,
        in_specs=[vmem] * 6,
        out_specs=(vmem, pl.BlockSpec(memory_space=pltpu.SMEM), vmem, vmem, vmem),
        scratch_shapes=scratch,
        compiler_params=pltpu.CompilerParams(
            collective_id=0, has_side_effects=True, vmem_limit_bytes=62 * 1024 * 1024
        ),
        cost_estimate=pl.CostEstimate(
            flops=2 * 2 * TOKENS * 2 * HD * HF, bytes_accessed=4 * 1024 * 1024, transcendentals=0
        ),
    )(
        hidden, weight, scale_param.reshape(1, 2 * HF), clip_upper.reshape(2, 128),
        clip_lower.reshape(2, 128), target,
    )
    approx, loss, gu, gl, gs = pl.pallas_call(
        hand_over,
        out_shape=shapes,
        in_specs=[vmem] * 5,
        out_specs=(vmem,) * 5,
    )(*results)
    return (
        approx, loss.reshape(()), gu.reshape(HD), gl.reshape(HD), gs.reshape(2 * HF)
    )


def solution(mesh):
    in_specs = (P("dp", "mp"), P("mp", "dp"), P("mp"), P("dp"), P("dp"), P("mp", "dp"))
    out_specs = (P("mp", "dp"), P(), P("dp"), P("dp"), P("mp"))
    return jax.shard_map(
        per_device, mesh=mesh, in_specs=in_specs, out_specs=out_specs, check_vma=False
    )
```

```python
import functools
import math

import jax
import jax.numpy as jnp
import numpy as np
from jax import lax
from jax.experimental import pallas as pl
from jax.experimental.pallas import tpu as pltpu
from jax.sharding import PartitionSpec as P

D = 8192
FF_W = 16384
TOKENS = 4096

X = 4
Z = 8
G = 4
TB = 32
HF = 1024
HD = 256
GT = X * X * 2 * TB
ZB = GT // Z
NH = 2
ZH = ZB // NH
COLUMN = 2 * Z
PLANE = X * X

f32 = jnp.float32
bf16 = jnp.bfloat16
MESH = pl.DeviceIdType.MESH


def rem(a, n):
    return lax.rem(a, jnp.int32(n))


def div(a, n):
    return lax.div(a, jnp.int32(n))


def in_squares(values, terms):
    nodes = 0.125 + 0.125 * np.cos(np.pi * (np.arange(64) + 0.5) / 64)
    fit = np.polynomial.chebyshev.Chebyshev.fit(nodes, values(nodes), terms - 1, domain=[0.0, 0.25])
    return [float(v) for v in fit.convert(kind=np.polynomial.Polynomial).coef[::-1]]


SINE = in_squares(lambda u: np.sin(2 * np.pi * np.sqrt(u)) / np.sqrt(u), 6)
COSINE = in_squares(lambda u: np.cos(2 * np.pi * np.sqrt(u)), 6)


def horner(coefs, u):
    v = coefs[0]
    for k in coefs[1:]:
        v = v * u + k
    return v


def kernel(
    hid_in, wgt_in, scl, cu, cl, tgt_in,
    apx, loss, gu_o, gl_o, gs_o,
    hid, wgt, tgt, in_sem, hall, hstage, wpeer, clipb, scol, wq, tU, tL, tS, red, colv, stat, part, pst, prc,
    sl, rl, ss, rs, eT, acc, gsacc, lacc, lossb, gradb, planeb, gsp,
    agS, agR, hxS, hxR, msS, msR, pS, pR, lS, lR, shS, shR, elS, elR, esS, esR, epS, epR,
    stS, stR, loS, loR, grS, grR, plS, plR,
):
    dp = lax.axis_index("dp")
    z = lax.axis_index("mp")
    c = rem(dp, 2)
    chip = div(dp, 2)
    x = div(chip, X)
    y = rem(chip, X)
    s = 1 - 2 * c
    column = z * 2 + c
    peer = (chip * 2 + 1 - c, z)
    around = {r: rem(z + Z + r * s, Z) for r in range(-4, 5)}

    def remote(src, dst, send, recv, device):
        return pltpu.make_async_remote_copy(
            src_ref=src, dst_ref=dst, send_sem=send, recv_sem=recv,
            device_id=device, device_id_type=MESH,
        )

    def in_column(o):
        other = rem(column + o, COLUMN)
        return (chip * 2 + rem(other, 2), div(other, 2))

    def in_plane(o):
        return (rem(chip + o, PLANE) * 2 + c, z)

    loads = [
        pltpu.make_async_copy(src, dst, in_sem.at[n])
        for n, (src, dst) in enumerate(((hid_in, hid), (wgt_in, wgt), (tgt_in, tgt)))
    ]
    for load in loads:
        load.start()

    barrier = pltpu.get_barrier_semaphore()

    def greet(o, carry):
        pl.semaphore_signal(barrier, inc=1, device_id=in_column(o), device_id_type=MESH)
        pl.semaphore_signal(barrier, inc=1, device_id=in_plane(o), device_id_type=MESH)
        return carry

    lax.fori_loop(1, COLUMN, greet, 0)
    pl.semaphore_wait(barrier, COLUMN - 1 + PLANE - 1)

    mine = pl.ds(pl.multiple_of(c * HF, HF), HF)
    theirs = pl.ds(pl.multiple_of((1 - c) * HF, HF), HF)

    def h_copy(g):
        return remote(
            hstage.at[pl.ds(pl.multiple_of(g * TB, TB), TB), :], hall.at[g, x, y, c],
            hxS.at[g], hxR.at[g], peer,
        )

    def scale_hidden(g, carry):
        rows = pl.ds(pl.multiple_of(g * TB, TB), TB)
        there = (hid[rows, theirs].astype(f32) / scl[:, theirs]).astype(bf16)
        hstage[rows, :] = there
        h_copy(g).start()
        here = (hid[rows, mine].astype(f32) / scl[:, mine]).astype(bf16)
        hall[g, x, y, c] = here
        return carry

    loads[0].wait()
    scale_hidden(0, 0)
    loads[1].wait()
    w_copy = remote(wgt.at[theirs, :], wpeer, msS.at[0], msR.at[0], peer)
    w_copy.start()
    for b in range(2):
        clipb[c, b:b + 1, :] = cu[b:b + 1, :]
        clipb[c, 2 + b:3 + b, :] = cl[b:b + 1, :]
    clip_copy = remote(clipb.at[c], clipb.at[c], msS.at[1], msR.at[1], peer)
    clip_copy.start()

    def h_wait(g):
        slot = hall.at[g, x, y, 1 - c]
        remote(slot, slot, hxS.at[g], hxR.at[g], peer).wait_recv()

    xs = {o: rem(x + X + o * s, X) for o in (0, -1, 1, 2)}
    ys = {o: rem(y + X + o * s, X) for o in (0, -1, 1, 2)}
    x_way = {o: (xs[o] * X + y) * 2 + c for o in (-1, 1)}
    y_way = {o: (x * X + ys[o]) * 2 + c for o in (-1, 1)}

    def block(g, b, p, q):
        return hall.at[g, xs[p], ys[q], 0] if b == 0 else hall.at[g, xs[q], ys[p], 1]

    routes = [(0, 0, 0, 1, -1, 0), (0, 0, 0, -1, 1, 0), (-1, 0, 0, 1, 2, 0)]
    for p in (0, -1, 1, 2):
        routes += [(p, 0, 1, 1, p, -1), (p, 0, 1, -1, p, 1), (p, -1, 1, 1, p, 2)]

    def ag_start(g, b, k):
        p, q, axis, way, _, _ = routes[k]
        src = block(g, b, p, q)
        to = (x_way if axis == b else y_way)[way]
        remote(src, src, agS.at[g, b, k], agR.at[g, b, k], (to, z)).start()

    def ag_wait(g, b, k):
        dst = block(g, b, routes[k][4], routes[k][5])
        remote(dst, dst, agS.at[g, b, k], agR.at[g, b, k], peer).wait_recv()

    def ag_step(g, arrived, onward):
        for b in range(2):
            for k in arrived:
                ag_wait(g, b, k)
            for k in onward:
                ag_start(g, b, k)

    def ag_0(g):
        h_wait(g)
        ag_step(g, (), (0, 1))

    def ag_1(g):
        ag_step(g, (0,), (2,))
        ag_step(g, (), (3, 4, 6, 7))

    def ag_2(g):
        ag_step(g, (1,), (9, 10))
        ag_step(g, (2,), (12, 13))

    def ag_3(g):
        for k in (3, 6, 9, 12):
            ag_step(g, (k,), (k + 2,))

    def ag_4(g):
        ag_step(g, (4, 7, 10, 13, 5, 8, 11, 14), ())

    def ag_sent(g):
        def one(k, carry):
            for b in range(2):
                src = block(g, b, 0, 0)
                remote(src, src, agS.at[g, b, k], agR.at[g, b, k], peer).wait_send()
            return carry

        lax.fori_loop(0, 15, one, 0)

    for k in range(2 * HF // 128):
        lanes = slice(128 * k, 128 * k + 128)
        scol[lanes, :] = jnp.broadcast_to(scl[:, lanes], (128, 128)).T

    ag_0(0)

    def extremes(k, carry):
        rows = pl.ds(pl.multiple_of(k * 64, 64), 64)
        ws = wgt[rows, :].astype(f32) * jnp.concatenate([scol[rows, :]] * 2, axis=1)
        ws = ws.reshape(8, 8, HD)
        return jnp.maximum(carry[0], jnp.max(ws, axis=0)), jnp.minimum(carry[1], jnp.min(ws, axis=0))

    top, bottom = lax.fori_loop(
        0, 2 * HF // 64, extremes, (jnp.full((8, HD), -jnp.inf, f32), jnp.full((8, HD), jnp.inf, f32))
    )
    top = jnp.max(top, axis=0, keepdims=True)
    bottom = jnp.min(bottom, axis=0, keepdims=True)
    for r in range(2):
        stat[column, r:r + 1, :] = top[:, 128 * r:128 * r + 128]
        stat[column, 2 + r:3 + r, :] = bottom[:, 128 * r:128 * r + 128]

    def column_send(buf, send, recv):
        def one(o, carry):
            remote(buf.at[column], buf.at[column], send.at[o - 1], recv.at[o - 1], in_column(o)).start()
            return carry
        lax.fori_loop(1, COLUMN, one, 0)

    def column_wait(buf, send, recv):
        def one(o, carry):
            src = buf.at[rem(column + COLUMN - o, COLUMN)]
            remote(src, src, send.at[o - 1], recv.at[o - 1], peer).wait_recv()
            return carry
        lax.fori_loop(1, COLUMN, one, 0)

    def column_sent(buf, send, recv):
        def one(o, carry):
            src = buf.at[column]
            remote(src, src, send.at[o - 1], recv.at[o - 1], peer).wait_send()
            return carry
        lax.fori_loop(1, COLUMN, one, 0)

    column_send(stat, stS, stR)
    lax.fori_loop(1, G, scale_hidden, 0)
    loads[2].wait()
    ag_1(0)

    lacc[...] = jnp.zeros_like(lacc)
    acc[...] = jnp.zeros_like(acc)
    gsacc[...] = jnp.zeros_like(gsacc)

    clip_other = clipb.at[1 - c]
    remote(clip_other, clip_other, msS.at[1], msR.at[1], peer).wait_recv()
    column_wait(stat, stS, stR)
    every = stat[...].reshape(Z, 2, 8, 128)
    col_max = jnp.max(every[:, :, 0:2, :], axis=0).reshape(4, 128)
    col_min = jnp.min(every[:, :, 2:4, :], axis=0).reshape(4, 128)
    sig_u = jax.nn.sigmoid(jnp.concatenate([clipb[0, 0:2, :], clipb[1, 0:2, :]], axis=0))
    sig_l = jax.nn.sigmoid(jnp.concatenate([clipb[0, 2:4, :], clipb[1, 2:4, :]], axis=0))
    lower = sig_l * col_min
    stepsize = (sig_u * col_max - lower + 1e-05) / 15.0
    inverse = 1.0 / stepsize
    first = c == 0

    def own_rows(v):
        return jnp.where(first, v[0:2], v[2:4])

    def other_rows(v):
        return jnp.where(first, v[2:4], v[0:2])

    def levels(ws, lo, inv):
        raw = (ws - lo) * inv
        level = jnp.clip(raw, 0.0, 15.0)
        turn = level - jnp.floor(level + 0.5)
        square = turn * turn
        soft = level - turn * horner([v * (0.8 / (2.0 * math.pi)) for v in SINE], square)
        return raw, level, square, soft

    STRIP = 16

    def quantize(src, row0, half, pick):
        lo, inv, st = pick(lower), pick(inverse), pick(stepsize)

        def one(k, carry):
            rows = pl.ds(pl.multiple_of(k * STRIP, STRIP), STRIP)
            sc = scol[pl.ds(pl.multiple_of(c * HF + k * STRIP, STRIP), STRIP), :]
            w = src[pl.ds(pl.multiple_of(row0 + k * STRIP, STRIP), STRIP), :].astype(f32)
            for r in range(2):
                lanes = slice(128 * r, 128 * r + 128)
                _, _, _, soft = levels(w[:, lanes] * sc, lo[r:r + 1], inv[r:r + 1])
                wq[rows, half * HD + 128 * r:half * HD + 128 * r + 128] = (st[r:r + 1] * soft + lo[r:r + 1]).astype(bf16)
            return carry

        lax.fori_loop(0, HF // STRIP, one, 0)

    ag_2(0)
    ag_0(1)
    quantize(wgt, c * HF, 1, own_rows)
    ag_3(0)
    w_copy.wait_recv()
    quantize(wpeer, 0, 0, other_rows)
    ag_1(1)
    ag_2(1)

    def columns():
        for r in range(4):
            rows = slice(128 * r, 128 * r + 128)
            for n, v in enumerate((lower, stepsize, inverse)):
                colv[n, rows, :] = jnp.broadcast_to(v[r:r + 1, :], (128, 128)).T

    def coefficients(k):
        lanes = pl.ds(pl.multiple_of(k * 128, 128), 128)
        sc = scl[:, pl.ds(pl.multiple_of(c * HF + k * 128, 128), 128)]
        rsc = 1.0 / sc
        for src, row0, core in ((wgt, c * HF, c), (wpeer, 0, 1 - c)):
            rows = pl.ds(pl.multiple_of(core * HD, HD), HD)
            tU[rows, lanes] = src[pl.ds(pl.multiple_of(row0 + k * 128, 128), 128), :].astype(f32).T

        def one(n, carry):
            rows = pl.ds(pl.multiple_of(n * 32, 32), 32)
            w = tU[rows, lanes]
            lo = colv[0, rows, :]
            raw, level, square, soft = levels(w * sc, lo, colv[2, rows, :])
            tie = jnp.where((raw == 0.0) | (raw == 15.0), 0.5, 1.0)
            inside = jnp.where(raw == level, tie, 0.0)
            slope = inside * (1.0 - 0.8 * horner(COSINE, square))
            q = (colv[1, rows, :] * soft + lo).astype(bf16).astype(f32)
            up = (soft - slope * level) * (1.0 / 15.0)
            tU[rows, lanes] = up
            tL[rows, lanes] = 1.0 - slope - up
            tS[rows, lanes] = slope * w - q * rsc
            return carry

        lax.fori_loop(0, 2 * HD // 32, one, 0)

    own_half = pl.ds(pl.multiple_of(c * HD, HD), HD)
    segments = [(jj * 2 * G * TB + b * G * TB, (2 * jj + b) * TB) for jj in range(2) for b in range(2)]
    MT = GT // 2

    def p_copy(g, t):
        part_of = pl.ds(4 * t, 4)
        return remote(pst.at[g, part_of], prc.at[g, part_of], pS.at[g, t], pR.at[g, t], peer)

    def forward(g):
        def one(t, carry):
            h = hall[g, pl.ds(2 * t, 2)].reshape(MT, HF)
            r = jnp.dot(h, wq[...], preferred_element_type=f32)
            for n in range(4):
                rows = slice(n * ZB, n * ZB + ZB)
                pst[g, 4 * t + n] = r[rows, :HD].astype(bf16)
                part[rem(g, 3), 4 * t + n] = r[rows, HD:]
            p_copy(g, t).start()
            return carry

        lax.fori_loop(0, 2, one, 0)

    def zcopy(src, dst, send, recv, to):
        return remote(src, dst, send, recv, (dp, to))

    def long_copy(g, m, h):
        n = (g, m - 1, h)
        return zcopy(sl.at[n], rl.at[n], lS.at[n], lR.at[n], around[1])

    def short_copy(g, m, h):
        n = (g, m - 1, h)
        return zcopy(ss.at[n], rs.at[n], shS.at[n], shR.at[n], around[-1])

    def total(g, block, h):
        rows = slice(h * ZH, h * ZH + ZH)
        return part[rem(g, 3), block, rows, :] + prc[g, block, rows, :].astype(f32)

    def sum_step(g, m):
        if m == 1:
            for t in range(2):
                p_copy(g, t).wait_recv()
        for h in range(NH):
            v = total(g, around[5 - m], h)
            w = total(g, around[m - 4], h) if m < 4 else None
            if m > 1:
                long_copy(g, m - 1, h).wait_recv()
                v = v + rl[g, m - 2, h].astype(f32)
            sl[g, m - 1, h] = v.astype(bf16)
            long_copy(g, m, h).start()
            if m < 4:
                if m > 1:
                    short_copy(g, m - 1, h).wait_recv()
                    w = w + rs[g, m - 2, h].astype(f32)
                ss[g, m - 1, h] = w.astype(bf16)
                short_copy(g, m, h).start()

    def eslot(g, block, core):
        return eT.at[g, block, pl.ds(pl.multiple_of(core * HD, HD), HD), :]

    def ehalf(g, block, h):
        return eT.at[g, block, pl.ds(pl.multiple_of(c * HD + h * (HD // NH), HD // NH), HD // NH), :]

    def long_err(g, m, h, recv=False):
        e = ehalf(g, around[-m if recv else 1 - m], h)
        return zcopy(e, e, elS.at[g, m - 1, h], elR.at[g, m - 1, h], around[1])

    def short_err(g, m, h, recv=False):
        e = ehalf(g, around[m if recv else m - 1], h)
        return zcopy(e, e, esS.at[g, m - 1, h], esR.at[g, m - 1, h], around[-1])

    def peer_err(g, block, core):
        e = eslot(g, block, core)
        return remote(e, e, epS.at[g, block], epR.at[g, block], peer)

    def err_step(g, m):
        for h in range(NH):
            long_err(g, m, h, True).wait_recv()
            if m < 4:
                long_err(g, m + 1, h).start()
                short_err(g, m, h, True).wait_recv()
                if m < 3:
                    short_err(g, m + 1, h).start()
        peer_err(g, around[-m], c).start()
        if m < 4:
            peer_err(g, around[m], c).start()

    def sum_end(g):
        for h in range(NH):
            long_copy(g, 4, h).wait_recv()
            short_copy(g, 3, h).wait_recv()
        v = jnp.concatenate(
            [total(g, z, h) + rl[g, 3, h].astype(f32) + rs[g, 2, h].astype(f32) for h in range(NH)], axis=0
        )
        goal = jnp.concatenate(
            [tgt[pl.ds(pl.multiple_of(first + g * TB, TB), TB), :] for first, _ in segments], axis=0
        ).astype(f32)
        err = v - goal
        eT[g, z, own_half, :] = err.T.astype(bf16)
        for h in range(NH):
            long_err(g, 1, h).start()
            short_err(g, 1, h).start()
        peer_err(g, z, c).start()
        lacc[...] += jnp.sum((err * err).reshape(ZB // 8, 8, HD), axis=0)
        back = v.astype(bf16)
        for first, at_row in segments:
            apx[pl.ds(pl.multiple_of(first + g * TB, TB), TB), :] = back[at_row:at_row + TB, :]

    def backward(g, offsets):
        blocks = [around[o] for o in offsets]
        for b in blocks:
            peer_err(g, b, 1 - c).wait_recv()

        def one(k, carry):
            lanes = pl.ds(pl.multiple_of(k * 512, 512), 512)
            e = jnp.concatenate([eT[g, b] for b in blocks], axis=1)
            h = jnp.concatenate(
                [hall[g, div(b, 2), pl.ds(2 * rem(b, 2), 2), :, :, lanes].reshape(ZB, 512) for b in blocks], axis=0
            )
            acc[:, lanes] += jnp.dot(e, h, preferred_element_type=f32)
            return carry

        lax.fori_loop(0, HF // 512, one, 0)

    def z_sent(g):
        for h in range(NH):
            for m in range(1, 5):
                long_copy(g, m, h).wait_send()
                long_err(g, m, h).wait_send()
            for m in range(1, 4):
                short_copy(g, m, h).wait_send()
                short_err(g, m, h).wait_send()
        for t in range(2):
            p_copy(g, t).wait_send()

        def one(block, carry):
            peer_err(g, block, c).wait_send()
            return carry

        lax.fori_loop(0, Z, one, 0)

    def turn_of(i, carry):
        def when(back, f, *more):
            g = i - back

            @pl.when((g >= 0) & (g < G))
            def _():
                f(g, *more)

        when(0, ag_4)
        when(0, forward)
        when(-2, ag_0)

        when(4, err_step, 4)
        when(3, err_step, 2)
        when(2, sum_end)
        when(1, sum_step, 3)
        when(0, sum_step, 1)
        when(-1, ag_3)
        when(4, backward, (3, -3, -4))
        when(-2, ag_1)

        @pl.when(i == G + 1)
        def _():
            lossb[column] = lacc[:, 0:128] + lacc[:, 128:256]
            column_send(lossb, loS, loR)

        @pl.when(i == 0)
        def _():
            columns()

        @pl.when(i < 4)
        def _():
            coefficients(2 * i)

        when(3, err_step, 3)
        when(2, err_step, 1)
        when(1, sum_step, 4)
        when(0, sum_step, 2)

        @pl.when(i < 4)
        def _():
            coefficients(2 * i + 1)

        when(-2, ag_2)
        when(3, backward, (0, 1, -1, 2, -2))

        @pl.when((i >= 5) & (i < G + 3))
        def _():
            ag_sent(i - 5)
            z_sent(i - 5)

        return carry

    lax.fori_loop(0, G + 3, turn_of, 0)
    column_wait(lossb, loS, loR)
    err_step(G - 1, 4)
    backward(G - 1, (3, -3, -4))
    def pull(a, carry):
        rows = pl.ds(pl.multiple_of(a * 64, 64), 64)
        up = jnp.zeros((64, 128), f32)
        low = jnp.zeros((64, 128), f32)
        for k in range(HF // 128):
            lanes = slice(128 * k, 128 * k + 128)
            g = acc[rows, lanes]
            up = up + g * tU[rows, lanes]
            low = low + g * tL[rows, lanes]
            gsacc[:, lanes] += jnp.sum((g * tS[rows, lanes]).reshape(8, 8, 128), axis=0)
        red[0, rows, :] = up
        red[1, rows, :] = low
        return carry

    lax.fori_loop(0, 2 * HD // 64, pull, 0)
    planeb[chip, 8:16, :] = jnp.sum(lossb[...], axis=0)
    gs_row = jnp.sum(gsacc[...], axis=0, keepdims=True)
    for k in range(HF // 128):
        planeb[chip, k:k + 1, :] = gs_row[:, 128 * k:128 * k + 128]

    def plane_copy(o, from_chip, device):
        src = planeb.at[from_chip]
        return remote(src, src, plS.at[o - 1], plR.at[o - 1], device)

    def plane_start(o, carry):
        plane_copy(o, chip, in_plane(o)).start()
        return carry

    lax.fori_loop(1, PLANE, plane_start, 0)

    for r in range(4):
        rows = slice(128 * r, 128 * r + 128)
        gradb[column, r:r + 1, :] = jnp.sum(red[0, rows, :].T, axis=0, keepdims=True)
        gradb[column, 4 + r:5 + r, :] = jnp.sum(red[1, rows, :].T, axis=0, keepdims=True)
    column_send(gradb, grS, grR)

    w_copy.wait_send()
    clip_copy.wait_send()

    def sent(g, carry):
        h_copy(g).wait_send()
        return carry

    lax.fori_loop(0, G, sent, 0)
    for g in range(G - 2, G):
        ag_sent(g)
        z_sent(g)
    column_sent(stat, stS, stR)
    column_sent(lossb, loS, loR)

    def plane_wait(o, carry):
        plane_copy(o, rem(chip + PLANE - o, PLANE), peer).wait_recv()
        return carry

    lax.fori_loop(1, PLANE, plane_wait, 0)
    whole = jnp.sum(planeb[...], axis=0)
    gsp[c] = whole[0:8, :]
    gs_copy = remote(gsp.at[c], gsp.at[c], msS.at[2], msR.at[2], peer)
    gs_copy.start()
    loss[0, 0] = jnp.sum(whole[8:16, :]) * (1.0 / (TOKENS * D))

    column_wait(gradb, grS, grR)
    grads = jnp.sum(gradb[...], axis=0)
    su = own_rows(sig_u)
    sd = own_rows(sig_l)
    gu_o[...] = (
        jnp.where(first, grads[0:2], grads[2:4])
        * own_rows(col_max) * (su * (1.0 - su))
    )
    gl_o[...] = (
        jnp.where(first, grads[4:6], grads[6:8])
        * own_rows(col_min) * (sd * (1.0 - sd))
    )
    column_sent(gradb, grS, grR)

    def plane_sent(o, carry):
        plane_copy(o, chip, peer).wait_send()
        return carry

    lax.fori_loop(1, PLANE, plane_sent, 0)
    gs_other = gsp.at[1 - c]
    remote(gs_other, gs_other, msS.at[2], msR.at[2], peer).wait_recv()
    gs_copy.wait_send()
    gs_o[0:8, :] = gsp[0]
    gs_o[8:16, :] = gsp[1]


def hand_over(*refs):
    n = len(refs) // 2
    for i in range(n):
        refs[n + i][...] = refs[i][...]


def per_device(hidden, weight, scale_param, clip_upper, clip_lower, target):
    vmem = pl.BlockSpec(memory_space=pltpu.VMEM)
    anywhere = pl.BlockSpec(memory_space=pl.ANY)
    dma = pltpu.SemaphoreType.DMA
    scratch = [
        pltpu.VMEM(hidden.shape, bf16),
        pltpu.VMEM(weight.shape, bf16),
        pltpu.VMEM(target.shape, bf16),
        dma((3,)),
        pltpu.VMEM((G, X, X, 2, TB, HF), bf16),
        pltpu.VMEM((G * TB, HF), bf16),
        pltpu.VMEM((HF, HD), bf16),
        pltpu.VMEM((2, 8, 128), f32),
        pltpu.VMEM((2 * HF, 128), f32),
        pltpu.VMEM((HF, 2 * HD), bf16),
        pltpu.VMEM((2 * HD, HF), f32),
        pltpu.VMEM((2 * HD, HF), f32),
        pltpu.VMEM((2 * HD, HF), f32),
        pltpu.VMEM((2, 2 * HD, 128), f32),
        pltpu.VMEM((3, 2 * HD, 128), f32),
        pltpu.VMEM((COLUMN, 8, 128), f32),
        pltpu.VMEM((3, Z, ZB, HD), f32),
        pltpu.VMEM((G, Z, ZB, HD), bf16),
        pltpu.VMEM((G, Z, ZB, HD), bf16),
        pltpu.VMEM((G, 4, NH, ZH, HD), bf16),
        pltpu.VMEM((G, 4, NH, ZH, HD), bf16),
        pltpu.VMEM((G, 3, NH, ZH, HD), bf16),
        pltpu.VMEM((G, 3, NH, ZH, HD), bf16),
        pltpu.VMEM((G, Z, 2 * HD, ZB), bf16),
        pltpu.VMEM((2 * HD, HF), f32),
        pltpu.VMEM((8, HF), f32),
        pltpu.VMEM((8, HD), f32),
        pltpu.VMEM((COLUMN, 8, 128), f32),
        pltpu.VMEM((COLUMN, 8, 128), f32),
        pltpu.VMEM((PLANE, 16, 128), f32),
        pltpu.VMEM((2, 8, 128), f32),
    ]
    for shape in (
        (G, 2, 15), (G,), (3,), (G, 2), (G, 4, NH), (G, 3, NH), (G, 4, NH), (G, 3, NH), (G, Z),
        (COLUMN - 1,), (COLUMN - 1,), (COLUMN - 1,), (PLANE - 1,),
    ):
        scratch += [dma(shape), dma(shape)]
    shapes = (
        jax.ShapeDtypeStruct((TOKENS // Z, HD), bf16),
        jax.ShapeDtypeStruct((1, 1), f32),
        jax.ShapeDtypeStruct((2, 128), f32),
        jax.ShapeDtypeStruct((2, 128), f32),
        jax.ShapeDtypeStruct((16, 128), f32),
    )
    results = pl.pallas_call(
        kernel,
        out_shape=shapes,
        in_specs=[anywhere, anywhere, vmem, vmem, vmem, anywhere],
        out_specs=(vmem, pl.BlockSpec(memory_space=pltpu.SMEM), vmem, vmem, vmem),
        scratch_shapes=scratch,
        compiler_params=pltpu.CompilerParams(
            collective_id=0, has_side_effects=True, vmem_limit_bytes=62 * 1024 * 1024
        ),
        cost_estimate=pl.CostEstimate(
            flops=2 * 2 * TOKENS * 2 * HD * HF, bytes_accessed=4 * 1024 * 1024, transcendentals=0
        ),
    )(
        hidden, weight, scale_param.reshape(1, 2 * HF), clip_upper.reshape(2, 128),
        clip_lower.reshape(2, 128), target,
    )
    approx, loss, gu, gl, gs = pl.pallas_call(
        hand_over,
        out_shape=shapes,
        in_specs=[vmem] * 5,
        out_specs=(vmem,) * 5,
    )(*results)
    return (
        approx, loss.reshape(()), gu.reshape(HD), gl.reshape(HD), gs.reshape(2 * HF)
    )


def solution(mesh):
    in_specs = (P("dp", "mp"), P("mp", "dp"), P("mp"), P("dp"), P("dp"), P("mp", "dp"))
    out_specs = (P("mp", "dp"), P(), P("dp"), P("dp"), P("mp"))
    return jax.shard_map(
        per_device, mesh=mesh, in_specs=in_specs, out_specs=out_specs, check_vma=False
    )
```

```python
import functools
import math

import jax
import jax.numpy as jnp
import numpy as np
from jax import lax
from jax.experimental import pallas as pl
from jax.experimental.pallas import tpu as pltpu
from jax.sharding import PartitionSpec as P

D = 8192
FF_W = 16384
TOKENS = 4096

X = 4
Z = 8
G = 4
TB = 32
HF = 1024
HD = 256
GT = X * X * 2 * TB
ZB = GT // Z
NH = 2
ZH = ZB // NH
COLUMN = 2 * Z
PLANE = X * X

f32 = jnp.float32
bf16 = jnp.bfloat16
MESH = pl.DeviceIdType.MESH


def rem(a, n):
    return lax.rem(a, jnp.int32(n))


def div(a, n):
    return lax.div(a, jnp.int32(n))


def in_squares(values, terms):
    nodes = 0.125 + 0.125 * np.cos(np.pi * (np.arange(64) + 0.5) / 64)
    fit = np.polynomial.chebyshev.Chebyshev.fit(nodes, values(nodes), terms - 1, domain=[0.0, 0.25])
    return [float(v) for v in fit.convert(kind=np.polynomial.Polynomial).coef[::-1]]


SINE = in_squares(lambda u: np.sin(2 * np.pi * np.sqrt(u)) / np.sqrt(u), 6)
COSINE = in_squares(lambda u: np.cos(2 * np.pi * np.sqrt(u)), 6)


def horner(coefs, u):
    v = coefs[0]
    for k in coefs[1:]:
        v = v * u + k
    return v


def kernel(
    hid_in, wgt_in, scl, cu, cl, tgt_in,
    apx, loss, gu_o, gl_o, gs_o,
    hid, wgt, tgt, in_sem, hall, hstage, wpeer, clipb, scol, wq, tU, tL, tS, red, colv, stat, part, pst, prc,
    sl, rl, ss, rs, eT, acc, gsacc, lacc, lossb, gradb, planeb, gsp,
    agS, agR, hxS, hxR, msS, msR, pS, pR, lS, lR, shS, shR, elS, elR, esS, esR, epS, epR,
    stS, stR, loS, loR, grS, grR, plS, plR,
):
    dp = lax.axis_index("dp")
    z = lax.axis_index("mp")
    c = rem(dp, 2)
    chip = div(dp, 2)
    x = div(chip, X)
    y = rem(chip, X)
    s = 1 - 2 * c
    column = z * 2 + c
    peer = (chip * 2 + 1 - c, z)
    around = {r: rem(z + Z + r * s, Z) for r in range(-4, 5)}

    def remote(src, dst, send, recv, device):
        return pltpu.make_async_remote_copy(
            src_ref=src, dst_ref=dst, send_sem=send, recv_sem=recv,
            device_id=device, device_id_type=MESH,
        )

    def in_column(o):
        other = rem(column + o, COLUMN)
        return (chip * 2 + rem(other, 2), div(other, 2))

    def in_plane(o):
        return (rem(chip + o, PLANE) * 2 + c, z)

    loads = [
        pltpu.make_async_copy(src, dst, in_sem.at[n])
        for n, (src, dst) in enumerate(((hid_in, hid), (wgt_in, wgt), (tgt_in, tgt)))
    ]
    for load in loads:
        load.start()

    barrier = pltpu.get_barrier_semaphore()

    def greet(o, carry):
        pl.semaphore_signal(barrier, inc=1, device_id=in_column(o), device_id_type=MESH)
        pl.semaphore_signal(barrier, inc=1, device_id=in_plane(o), device_id_type=MESH)
        return carry

    lax.fori_loop(1, COLUMN, greet, 0)
    pl.semaphore_wait(barrier, COLUMN - 1 + PLANE - 1)

    mine = pl.ds(pl.multiple_of(c * HF, HF), HF)
    theirs = pl.ds(pl.multiple_of((1 - c) * HF, HF), HF)

    def h_copy(g):
        return remote(
            hstage.at[pl.ds(pl.multiple_of(g * TB, TB), TB), :], hall.at[g, x, y, c],
            hxS.at[g], hxR.at[g], peer,
        )

    def scale_hidden(g, carry):
        rows = pl.ds(pl.multiple_of(g * TB, TB), TB)
        there = (hid[rows, theirs].astype(f32) / scl[:, theirs]).astype(bf16)
        hstage[rows, :] = there
        h_copy(g).start()
        here = (hid[rows, mine].astype(f32) / scl[:, mine]).astype(bf16)
        hall[g, x, y, c] = here
        return carry

    loads[0].wait()
    scale_hidden(0, 0)
    loads[1].wait()
    w_copy = remote(wgt.at[theirs, :], wpeer, msS.at[0], msR.at[0], peer)
    w_copy.start()
    for b in range(2):
        clipb[c, b:b + 1, :] = cu[b:b + 1, :]
        clipb[c, 2 + b:3 + b, :] = cl[b:b + 1, :]
    clip_copy = remote(clipb.at[c], clipb.at[c], msS.at[1], msR.at[1], peer)
    clip_copy.start()

    def h_wait(g):
        slot = hall.at[g, x, y, 1 - c]
        remote(slot, slot, hxS.at[g], hxR.at[g], peer).wait_recv()

    xs = {o: rem(x + X + o * s, X) for o in (0, -1, 1, 2)}
    ys = {o: rem(y + X + o * s, X) for o in (0, -1, 1, 2)}
    x_way = {o: (xs[o] * X + y) * 2 + c for o in (-1, 1)}
    y_way = {o: (x * X + ys[o]) * 2 + c for o in (-1, 1)}

    def block(g, b, p, q):
        return hall.at[g, xs[p], ys[q], 0] if b == 0 else hall.at[g, xs[q], ys[p], 1]

    routes = [(0, 0, 0, 1, -1, 0), (0, 0, 0, -1, 1, 0), (-1, 0, 0, 1, 2, 0)]
    for p in (0, -1, 1, 2):
        routes += [(p, 0, 1, 1, p, -1), (p, 0, 1, -1, p, 1), (p, -1, 1, 1, p, 2)]

    def ag_start(g, b, k):
        p, q, axis, way, _, _ = routes[k]
        src = block(g, b, p, q)
        to = (x_way if axis == b else y_way)[way]
        remote(src, src, agS.at[g, b, k], agR.at[g, b, k], (to, z)).start()

    def ag_wait(g, b, k):
        dst = block(g, b, routes[k][4], routes[k][5])
        remote(dst, dst, agS.at[g, b, k], agR.at[g, b, k], peer).wait_recv()

    def ag_step(g, arrived, onward):
        for b in range(2):
            for k in arrived:
                ag_wait(g, b, k)
            for k in onward:
                ag_start(g, b, k)

    def ag_0(g):
        h_wait(g)
        ag_step(g, (), (0, 1))

    def ag_1(g):
        ag_step(g, (0,), (2,))
        ag_step(g, (1,), (3, 4, 6, 7, 9, 10))

    def ag_2(g):
        ag_step(g, (2,), (12, 13))

    def ag_3(g):
        for k in (3, 6, 9, 12):
            ag_step(g, (k,), (k + 2,))

    def ag_4(g):
        ag_step(g, (4, 7, 10, 13, 5, 8, 11, 14), ())

    def ag_sent(g):
        def one(k, carry):
            for b in range(2):
                src = block(g, b, 0, 0)
                remote(src, src, agS.at[g, b, k], agR.at[g, b, k], peer).wait_send()
            return carry

        lax.fori_loop(0, 15, one, 0)

    for k in range(2 * HF // 128):
        lanes = slice(128 * k, 128 * k + 128)
        scol[lanes, :] = jnp.broadcast_to(scl[:, lanes], (128, 128)).T

    ag_0(0)

    def extremes(k, carry):
        rows = pl.ds(pl.multiple_of(k * 64, 64), 64)
        ws = wgt[rows, :].astype(f32) * jnp.concatenate([scol[rows, :]] * 2, axis=1)
        ws = ws.reshape(8, 8, HD)
        return jnp.maximum(carry[0], jnp.max(ws, axis=0)), jnp.minimum(carry[1], jnp.min(ws, axis=0))

    top, bottom = lax.fori_loop(
        0, 2 * HF // 64, extremes, (jnp.full((8, HD), -jnp.inf, f32), jnp.full((8, HD), jnp.inf, f32))
    )
    top = jnp.max(top, axis=0, keepdims=True)
    bottom = jnp.min(bottom, axis=0, keepdims=True)
    for r in range(2):
        stat[column, r:r + 1, :] = top[:, 128 * r:128 * r + 128]
        stat[column, 2 + r:3 + r, :] = bottom[:, 128 * r:128 * r + 128]

    def column_send(buf, send, recv):
        def one(o, carry):
            remote(buf.at[column], buf.at[column], send.at[o - 1], recv.at[o - 1], in_column(o)).start()
            return carry
        lax.fori_loop(1, COLUMN, one, 0)

    def column_wait(buf, send, recv):
        def one(o, carry):
            src = buf.at[rem(column + COLUMN - o, COLUMN)]
            remote(src, src, send.at[o - 1], recv.at[o - 1], peer).wait_recv()
            return carry
        lax.fori_loop(1, COLUMN, one, 0)

    def column_sent(buf, send, recv):
        def one(o, carry):
            src = buf.at[column]
            remote(src, src, send.at[o - 1], recv.at[o - 1], peer).wait_send()
            return carry
        lax.fori_loop(1, COLUMN, one, 0)

    column_send(stat, stS, stR)
    lax.fori_loop(1, G, scale_hidden, 0)
    loads[2].wait()
    ag_1(0)

    lacc[...] = jnp.zeros_like(lacc)
    acc[...] = jnp.zeros_like(acc)
    gsacc[...] = jnp.zeros_like(gsacc)

    clip_other = clipb.at[1 - c]
    remote(clip_other, clip_other, msS.at[1], msR.at[1], peer).wait_recv()
    column_wait(stat, stS, stR)
    every = stat[...].reshape(Z, 2, 8, 128)
    col_max = jnp.max(every[:, :, 0:2, :], axis=0).reshape(4, 128)
    col_min = jnp.min(every[:, :, 2:4, :], axis=0).reshape(4, 128)
    sig_u = jax.nn.sigmoid(jnp.concatenate([clipb[0, 0:2, :], clipb[1, 0:2, :]], axis=0))
    sig_l = jax.nn.sigmoid(jnp.concatenate([clipb[0, 2:4, :], clipb[1, 2:4, :]], axis=0))
    lower = sig_l * col_min
    stepsize = (sig_u * col_max - lower + 1e-05) / 15.0
    inverse = 1.0 / stepsize
    first = c == 0

    def own_rows(v):
        return jnp.where(first, v[0:2], v[2:4])

    def other_rows(v):
        return jnp.where(first, v[2:4], v[0:2])

    def levels(ws, lo, inv):
        raw = (ws - lo) * inv
        level = jnp.clip(raw, 0.0, 15.0)
        turn = level - jnp.floor(level + 0.5)
        square = turn * turn
        soft = level - turn * horner([v * (0.8 / (2.0 * math.pi)) for v in SINE], square)
        return raw, level, square, soft

    STRIP = 16

    def quantize(src, row0, half, pick):
        lo, inv, st = pick(lower), pick(inverse), pick(stepsize)

        def one(k, carry):
            rows = pl.ds(pl.multiple_of(k * STRIP, STRIP), STRIP)
            sc = scol[pl.ds(pl.multiple_of(c * HF + k * STRIP, STRIP), STRIP), :]
            w = src[pl.ds(pl.multiple_of(row0 + k * STRIP, STRIP), STRIP), :].astype(f32)
            for r in range(2):
                lanes = slice(128 * r, 128 * r + 128)
                _, _, _, soft = levels(w[:, lanes] * sc, lo[r:r + 1], inv[r:r + 1])
                wq[rows, half * HD + 128 * r:half * HD + 128 * r + 128] = (st[r:r + 1] * soft + lo[r:r + 1]).astype(bf16)
            return carry

        lax.fori_loop(0, HF // STRIP, one, 0)

    ag_2(0)
    ag_0(1)
    quantize(wgt, c * HF, 1, own_rows)
    ag_3(0)
    w_copy.wait_recv()
    quantize(wpeer, 0, 0, other_rows)
    ag_1(1)
    ag_2(1)

    def columns():
        for r in range(4):
            rows = slice(128 * r, 128 * r + 128)
            for n, v in enumerate((lower, stepsize, inverse)):
                colv[n, rows, :] = jnp.broadcast_to(v[r:r + 1, :], (128, 128)).T

    def coefficients(k):
        lanes = pl.ds(pl.multiple_of(k * 128, 128), 128)
        sc = scl[:, pl.ds(pl.multiple_of(c * HF + k * 128, 128), 128)]
        rsc = 1.0 / sc
        for src, row0, core in ((wgt, c * HF, c), (wpeer, 0, 1 - c)):
            rows = pl.ds(pl.multiple_of(core * HD, HD), HD)
            tU[rows, lanes] = src[pl.ds(pl.multiple_of(row0 + k * 128, 128), 128), :].astype(f32).T

        def one(n, carry):
            rows = pl.ds(pl.multiple_of(n * 32, 32), 32)
            w = tU[rows, lanes]
            lo = colv[0, rows, :]
            raw, level, square, soft = levels(w * sc, lo, colv[2, rows, :])
            tie = jnp.where((raw == 0.0) | (raw == 15.0), 0.5, 1.0)
            inside = jnp.where(raw == level, tie, 0.0)
            slope = inside * (1.0 - 0.8 * horner(COSINE, square))
            q = (colv[1, rows, :] * soft + lo).astype(bf16).astype(f32)
            up = (soft - slope * level) * (1.0 / 15.0)
            tU[rows, lanes] = up
            tL[rows, lanes] = 1.0 - slope - up
            tS[rows, lanes] = slope * w - q * rsc
            return carry

        lax.fori_loop(0, 2 * HD // 32, one, 0)

    own_half = pl.ds(pl.multiple_of(c * HD, HD), HD)
    segments = [(jj * 2 * G * TB + b * G * TB, (2 * jj + b) * TB) for jj in range(2) for b in range(2)]
    MT = GT // 2

    def p_copy(g, t):
        part_of = pl.ds(4 * t, 4)
        return remote(pst.at[g, part_of], prc.at[g, part_of], pS.at[g, t], pR.at[g, t], peer)

    def forward(g):
        def one(t, carry):
            h = hall[g, pl.ds(2 * t, 2)].reshape(MT, HF)
            r = jnp.dot(h, wq[...], preferred_element_type=f32)
            for n in range(4):
                rows = slice(n * ZB, n * ZB + ZB)
                pst[g, 4 * t + n] = r[rows, :HD].astype(bf16)
                part[rem(g, 3), 4 * t + n] = r[rows, HD:]
            p_copy(g, t).start()
            return carry

        lax.fori_loop(0, 2, one, 0)

    def zcopy(src, dst, send, recv, to):
        return remote(src, dst, send, recv, (dp, to))

    def long_copy(g, m, h):
        n = (g, m - 1, h)
        return zcopy(sl.at[n], rl.at[n], lS.at[n], lR.at[n], around[1])

    def short_copy(g, m, h):
        n = (g, m - 1, h)
        return zcopy(ss.at[n], rs.at[n], shS.at[n], shR.at[n], around[-1])

    def total(g, block, h):
        rows = slice(h * ZH, h * ZH + ZH)
        return part[rem(g, 3), block, rows, :] + prc[g, block, rows, :].astype(f32)

    def sum_step(g, m):
        if m == 1:
            for t in range(2):
                p_copy(g, t).wait_recv()
        for h in range(NH):
            v = total(g, around[5 - m], h)
            w = total(g, around[m - 4], h) if m < 4 else None
            if m > 1:
                long_copy(g, m - 1, h).wait_recv()
                v = v + rl[g, m - 2, h].astype(f32)
            sl[g, m - 1, h] = v.astype(bf16)
            long_copy(g, m, h).start()
            if m < 4:
                if m > 1:
                    short_copy(g, m - 1, h).wait_recv()
                    w = w + rs[g, m - 2, h].astype(f32)
                ss[g, m - 1, h] = w.astype(bf16)
                short_copy(g, m, h).start()

    def eslot(g, block, core):
        return eT.at[g, block, pl.ds(pl.multiple_of(core * HD, HD), HD), :]

    def ehalf(g, block, h):
        return eT.at[g, block, pl.ds(pl.multiple_of(c * HD + h * (HD // NH), HD // NH), HD // NH), :]

    def long_err(g, m, h, recv=False):
        e = ehalf(g, around[-m if recv else 1 - m], h)
        return zcopy(e, e, elS.at[g, m - 1, h], elR.at[g, m - 1, h], around[1])

    def short_err(g, m, h, recv=False):
        e = ehalf(g, around[m if recv else m - 1], h)
        return zcopy(e, e, esS.at[g, m - 1, h], esR.at[g, m - 1, h], around[-1])

    def peer_err(g, block, core):
        e = eslot(g, block, core)
        return remote(e, e, epS.at[g, block], epR.at[g, block], peer)

    def err_step(g, m):
        for h in range(NH):
            long_err(g, m, h, True).wait_recv()
            if m < 4:
                long_err(g, m + 1, h).start()
                short_err(g, m, h, True).wait_recv()
                if m < 3:
                    short_err(g, m + 1, h).start()
        peer_err(g, around[-m], c).start()
        if m < 4:
            peer_err(g, around[m], c).start()

    def sum_end(g):
        for h in range(NH):
            long_copy(g, 4, h).wait_recv()
            short_copy(g, 3, h).wait_recv()
        v = jnp.concatenate(
            [total(g, z, h) + rl[g, 3, h].astype(f32) + rs[g, 2, h].astype(f32) for h in range(NH)], axis=0
        )
        goal = jnp.concatenate(
            [tgt[pl.ds(pl.multiple_of(first + g * TB, TB), TB), :] for first, _ in segments], axis=0
        ).astype(f32)
        err = v - goal
        eT[g, z, own_half, :] = err.T.astype(bf16)
        for h in range(NH):
            long_err(g, 1, h).start()
            short_err(g, 1, h).start()
        peer_err(g, z, c).start()
        lacc[...] += jnp.sum((err * err).reshape(ZB // 8, 8, HD), axis=0)
        back = v.astype(bf16)
        for first, at_row in segments:
            apx[pl.ds(pl.multiple_of(first + g * TB, TB), TB), :] = back[at_row:at_row + TB, :]

    def backward(g, offsets):
        blocks = [around[o] for o in offsets]
        for b in blocks:
            peer_err(g, b, 1 - c).wait_recv()

        def one(k, carry):
            lanes = pl.ds(pl.multiple_of(k * 512, 512), 512)
            e = jnp.concatenate([eT[g, b] for b in blocks], axis=1)
            h = jnp.concatenate(
                [hall[g, div(b, 2), pl.ds(2 * rem(b, 2), 2), :, :, lanes].reshape(ZB, 512) for b in blocks], axis=0
            )
            acc[:, lanes] += jnp.dot(e, h, preferred_element_type=f32)
            return carry

        lax.fori_loop(0, HF // 512, one, 0)

    def z_sent(g):
        for h in range(NH):
            for m in range(1, 5):
                long_copy(g, m, h).wait_send()
                long_err(g, m, h).wait_send()
            for m in range(1, 4):
                short_copy(g, m, h).wait_send()
                short_err(g, m, h).wait_send()
        for t in range(2):
            p_copy(g, t).wait_send()

        def one(block, carry):
            peer_err(g, block, c).wait_send()
            return carry

        lax.fori_loop(0, Z, one, 0)

    def turn_of(i, carry):
        def when(back, f, *more):
            g = i - back

            @pl.when((g >= 0) & (g < G))
            def _():
                f(g, *more)

        when(0, ag_4)
        when(0, forward)
        when(-2, ag_0)

        when(4, err_step, 4)
        when(3, err_step, 2)
        when(2, sum_end)
        when(1, sum_step, 3)
        when(0, sum_step, 1)
        when(-1, ag_3)
        when(4, backward, (3, -3, -4))
        when(-2, ag_1)

        @pl.when(i == G + 1)
        def _():
            lossb[column] = lacc[:, 0:128] + lacc[:, 128:256]
            column_send(lossb, loS, loR)

        @pl.when(i == 0)
        def _():
            columns()

        @pl.when(i < 4)
        def _():
            coefficients(2 * i)

        when(3, err_step, 3)
        when(2, err_step, 1)
        when(1, sum_step, 4)
        when(0, sum_step, 2)

        @pl.when(i < 4)
        def _():
            coefficients(2 * i + 1)

        when(-2, ag_2)
        when(3, backward, (0, 1, -1, 2, -2))

        @pl.when((i >= 5) & (i < G + 3))
        def _():
            ag_sent(i - 5)
            z_sent(i - 5)

        return carry

    lax.fori_loop(0, G + 3, turn_of, 0)
    column_wait(lossb, loS, loR)
    err_step(G - 1, 4)
    backward(G - 1, (3, -3, -4))
    def pull(a, carry):
        rows = pl.ds(pl.multiple_of(a * 64, 64), 64)
        up = jnp.zeros((64, 128), f32)
        low = jnp.zeros((64, 128), f32)
        for k in range(HF // 128):
            lanes = slice(128 * k, 128 * k + 128)
            g = acc[rows, lanes]
            up = up + g * tU[rows, lanes]
            low = low + g * tL[rows, lanes]
            gsacc[:, lanes] += jnp.sum((g * tS[rows, lanes]).reshape(8, 8, 128), axis=0)
        red[0, rows, :] = up
        red[1, rows, :] = low
        return carry

    lax.fori_loop(0, 2 * HD // 64, pull, 0)
    planeb[chip, 8:16, :] = jnp.sum(lossb[...], axis=0)
    gs_row = jnp.sum(gsacc[...], axis=0, keepdims=True)
    for k in range(HF // 128):
        planeb[chip, k:k + 1, :] = gs_row[:, 128 * k:128 * k + 128]

    def plane_copy(o, from_chip, device):
        src = planeb.at[from_chip]
        return remote(src, src, plS.at[o - 1], plR.at[o - 1], device)

    def plane_start(o, carry):
        plane_copy(o, chip, in_plane(o)).start()
        return carry

    lax.fori_loop(1, PLANE, plane_start, 0)

    for r in range(4):
        rows = slice(128 * r, 128 * r + 128)
        gradb[column, r:r + 1, :] = jnp.sum(red[0, rows, :].T, axis=0, keepdims=True)
        gradb[column, 4 + r:5 + r, :] = jnp.sum(red[1, rows, :].T, axis=0, keepdims=True)
    column_send(gradb, grS, grR)

    w_copy.wait_send()
    clip_copy.wait_send()

    def sent(g, carry):
        h_copy(g).wait_send()
        return carry

    lax.fori_loop(0, G, sent, 0)
    for g in range(G - 2, G):
        ag_sent(g)
        z_sent(g)
    column_sent(stat, stS, stR)
    column_sent(lossb, loS, loR)

    def plane_wait(o, carry):
        plane_copy(o, rem(chip + PLANE - o, PLANE), peer).wait_recv()
        return carry

    lax.fori_loop(1, PLANE, plane_wait, 0)
    whole = jnp.sum(planeb[...], axis=0)
    gsp[c] = whole[0:8, :]
    gs_copy = remote(gsp.at[c], gsp.at[c], msS.at[2], msR.at[2], peer)
    gs_copy.start()
    loss[0, 0] = jnp.sum(whole[8:16, :]) * (1.0 / (TOKENS * D))

    column_wait(gradb, grS, grR)
    grads = jnp.sum(gradb[...], axis=0)
    su = own_rows(sig_u)
    sd = own_rows(sig_l)
    gu_o[...] = (
        jnp.where(first, grads[0:2], grads[2:4])
        * own_rows(col_max) * (su * (1.0 - su))
    )
    gl_o[...] = (
        jnp.where(first, grads[4:6], grads[6:8])
        * own_rows(col_min) * (sd * (1.0 - sd))
    )
    column_sent(gradb, grS, grR)

    def plane_sent(o, carry):
        plane_copy(o, chip, peer).wait_send()
        return carry

    lax.fori_loop(1, PLANE, plane_sent, 0)
    gs_other = gsp.at[1 - c]
    remote(gs_other, gs_other, msS.at[2], msR.at[2], peer).wait_recv()
    gs_copy.wait_send()
    gs_o[0:8, :] = gsp[0]
    gs_o[8:16, :] = gsp[1]


def hand_over(*refs):
    n = len(refs) // 2
    for i in range(n):
        refs[n + i][...] = refs[i][...]


def per_device(hidden, weight, scale_param, clip_upper, clip_lower, target):
    vmem = pl.BlockSpec(memory_space=pltpu.VMEM)
    anywhere = pl.BlockSpec(memory_space=pl.ANY)
    dma = pltpu.SemaphoreType.DMA
    scratch = [
        pltpu.VMEM(hidden.shape, bf16),
        pltpu.VMEM(weight.shape, bf16),
        pltpu.VMEM(target.shape, bf16),
        dma((3,)),
        pltpu.VMEM((G, X, X, 2, TB, HF), bf16),
        pltpu.VMEM((G * TB, HF), bf16),
        pltpu.VMEM((HF, HD), bf16),
        pltpu.VMEM((2, 8, 128), f32),
        pltpu.VMEM((2 * HF, 128), f32),
        pltpu.VMEM((HF, 2 * HD), bf16),
        pltpu.VMEM((2 * HD, HF), f32),
        pltpu.VMEM((2 * HD, HF), f32),
        pltpu.VMEM((2 * HD, HF), f32),
        pltpu.VMEM((2, 2 * HD, 128), f32),
        pltpu.VMEM((3, 2 * HD, 128), f32),
        pltpu.VMEM((COLUMN, 8, 128), f32),
        pltpu.VMEM((3, Z, ZB, HD), f32),
        pltpu.VMEM((G, Z, ZB, HD), bf16),
        pltpu.VMEM((G, Z, ZB, HD), bf16),
        pltpu.VMEM((G, 4, NH, ZH, HD), bf16),
        pltpu.VMEM((G, 4, NH, ZH, HD), bf16),
        pltpu.VMEM((G, 3, NH, ZH, HD), bf16),
        pltpu.VMEM((G, 3, NH, ZH, HD), bf16),
        pltpu.VMEM((G, Z, 2 * HD, ZB), bf16),
        pltpu.VMEM((2 * HD, HF), f32),
        pltpu.VMEM((8, HF), f32),
        pltpu.VMEM((8, HD), f32),
        pltpu.VMEM((COLUMN, 8, 128), f32),
        pltpu.VMEM((COLUMN, 8, 128), f32),
        pltpu.VMEM((PLANE, 16, 128), f32),
        pltpu.VMEM((2, 8, 128), f32),
    ]
    for shape in (
        (G, 2, 15), (G,), (3,), (G, 2), (G, 4, NH), (G, 3, NH), (G, 4, NH), (G, 3, NH), (G, Z),
        (COLUMN - 1,), (COLUMN - 1,), (COLUMN - 1,), (PLANE - 1,),
    ):
        scratch += [dma(shape), dma(shape)]
    shapes = (
        jax.ShapeDtypeStruct((TOKENS // Z, HD), bf16),
        jax.ShapeDtypeStruct((1, 1), f32),
        jax.ShapeDtypeStruct((2, 128), f32),
        jax.ShapeDtypeStruct((2, 128), f32),
        jax.ShapeDtypeStruct((16, 128), f32),
    )
    results = pl.pallas_call(
        kernel,
        out_shape=shapes,
        in_specs=[anywhere, anywhere, vmem, vmem, vmem, anywhere],
        out_specs=(vmem, pl.BlockSpec(memory_space=pltpu.SMEM), vmem, vmem, vmem),
        scratch_shapes=scratch,
        compiler_params=pltpu.CompilerParams(
            collective_id=0, has_side_effects=True, vmem_limit_bytes=62 * 1024 * 1024
        ),
        cost_estimate=pl.CostEstimate(
            flops=2 * 2 * TOKENS * 2 * HD * HF, bytes_accessed=4 * 1024 * 1024, transcendentals=0
        ),
    )(
        hidden, weight, scale_param.reshape(1, 2 * HF), clip_upper.reshape(2, 128),
        clip_lower.reshape(2, 128), target,
    )
    approx, loss, gu, gl, gs = pl.pallas_call(
        hand_over,
        out_shape=shapes,
        in_specs=[vmem] * 5,
        out_specs=(vmem,) * 5,
    )(*results)
    return (
        approx, loss.reshape(()), gu.reshape(HD), gl.reshape(HD), gs.reshape(2 * HF)
    )


def solution(mesh):
    in_specs = (P("dp", "mp"), P("mp", "dp"), P("mp"), P("dp"), P("dp"), P("mp", "dp"))
    out_specs = (P("mp", "dp"), P(), P("dp"), P("dp"), P("mp"))
    return jax.shard_map(
        per_device, mesh=mesh, in_specs=in_specs, out_specs=out_specs, check_vma=False
    )
```
